1024 devices in a mesh: dp: 4 (over y_hi), expert: 32 (over z, core), tensor: 8 (over x, y_lo).
Axes of the slice: x: 4, y: 8 (y_hi: 4, y_lo: 2; y = y_hi * 2 + y_lo), z: 16, core: 2. Of those that a mesh axis runs over, the one named last changes fastest.
Arguments:
- out_grad: bfloat16 [16384, 7168], P(('dp', 'expert'), 'tensor'), may hold values from -6 to 6
- expert_ids: int32 [16384, 2], P(('dp', 'expert')), may hold values from 0 to 63, all different within a row; in each aligned block of 128 rows (0 to 127, 128 to 255, ...) at most 6 rows name the same one
- gate_probs: float32 [16384, 2], P(('dp', 'expert')), may hold values from 0.1 to 1
- expert_down: bfloat16 [64, 2432, 7168], P('expert', 'dp', 'tensor'), may hold values from -0.0625 to 0.0625
- saved_gate: bfloat16 [64, 768, 2432], P('expert', 'tensor', 'dp'), may hold values from -6 to 6
- saved_up: bfloat16 [64, 768, 2432], P('expert', 'tensor', 'dp'), may hold values from -6 to 6
Outputs:
- grad_gate: bfloat16 [64, 768, 2432], P('expert', 'tensor', 'dp')
- grad_up: bfloat16 [64, 768, 2432], P('expert', 'tensor', 'dp')
The draws below stay inside these ranges and needn't reach their ends.
Inputs may be any that keep to these rules, and one draw needn't show every extreme that they name: `expert_ids`: within each group of 128 consecutive tokens (the tokens of one device), no expert is named by more than 6 entries, a bound that some block reaches; a token's two experts differ.
All inputs are finite; a program needn't handle non-finite values.
Results may differ from the reference program's by a relative error of at most 0.019.
Values may be sent and summed in bfloat16 or wider, within the bound.
A program may use at most 32 MiB of HBM per device.

```python
import math
import jax
import jax.numpy as jnp
import numpy as np
from jax import lax

D = 7168
EFF = 2432
EXPERTS = 64
TOK = 128
TOKENS = 16384
CAP = 6
SLOTS = 768
N_DP = 4
N_EXPERT = 32
N_TENSOR = 8


def block_levels(stream_key, shape, shards, least, high):
    def one(axis_at, shards_of):
        steps = jax.random.uniform(jax.random.fold_in(jax.random.fold_in(stream_key, 6), axis_at), (shards_of,), jnp.float32, least / len(shards), high / len(shards))
        return jnp.repeat(jnp.exp(steps), shape[axis_at] // shards_of).reshape((-1,) + (1,) * (len(shape) - axis_at - 1))

    factor_of = one(*shards[0])
    for cut in shards[1:]:
        factor_of = factor_of * one(*cut)
    return factor_of


def shared_out(stream_key, own, number, rows, count, top, reach, skew):
    sequence = jax.random.permutation(stream_key, count)
    packed, common = load_shares(count, rows * top, reach, skew, True), load_shares(count, rows * top, reach, skew, False)
    places = jnp.arange(count)

    def named(lengths, rotation):
        used = int((lengths > 0).sum())
        fixed = max(1, used // 4)
        moved = fixed + (places - fixed + rotation * (used - fixed)) % max(1, count - fixed)
        return jnp.zeros((count,), jnp.int32).at[sequence[jnp.where(places < fixed, places, moved)]].set(jnp.asarray(lengths, jnp.int32))

    lengths = jnp.where(number % 4 == 0, named(packed, number // 4), named(common, number - number // 4 - 1))
    mixed = jax.random.permutation(jax.random.fold_in(own, 3), count)
    donor, sink = mixed[0:count // 2 * 2:2], mixed[1:count // 2 * 2:2]
    margin = jnp.minimum(lengths[donor] - 1, reach - lengths[sink]) // 2
    margin = jnp.where((donor == sequence[0]) | (sink == sequence[0]) | (lengths[sink] == 0), 0, jnp.maximum(margin, 0))
    moved = jax.random.randint(jax.random.fold_in(own, 4), (count // 2,), 0, 1 << 20) % (margin + 1)
    lengths = lengths.at[donor].add(-moved).at[sink].add(moved)
    labels = jnp.searchsorted(jnp.cumsum(lengths), jnp.arange(rows * top), side="right").astype(jnp.int32)
    table = labels.reshape(top, rows).T
    table = table[jax.random.permutation(jax.random.fold_in(own, 1), rows)]
    rotation = jax.random.randint(jax.random.fold_in(own, 2), (rows, 1), 0, top)
    return jnp.take_along_axis(table, (jnp.arange(top)[None, :] + rotation) % top, axis=1)


def load_shares(amount, total, most, slope, full):
    weights = [(1 << 20) // math.isqrt(rank ** slope) + 1 for rank in range(1, amount + 1)]
    largest = most if full else min(most, max(-(-total // amount), total * weights[0] // sum(weights)))
    least = 1 if total - largest >= amount - 1 else 0
    counts, spare = [largest] + [least] * (amount - 1), total - largest - least * (amount - 1)
    while spare > 0:
        movable = [i for i in range(1, amount) if counts[i] < largest] or [i for i in range(1, amount) if counts[i] < most]
        mass, left = sum([weights[i] for i in movable]), spare
        for i in movable:
            more = min(most - counts[i], max(1, left * weights[i] // mass), spare)
            counts[i] = counts[i] + more
            spare = spare - more
    return np.array(counts)


def centred(own_key, shape, width, most, pieces=(), kind=jnp.bfloat16):
    values = width * jax.random.normal(own_key, shape, jnp.float32)
    if pieces:
        values = values * block_levels(own_key, shape, pieces, -0.22, 0.18)
    return jnp.clip(values, -most, most).astype(kind)


def setup_inputs(seed: int = 0) -> dict:
    streams_of = jax.random.split(jax.random.key(seed), 7)
    out_grad = centred(streams_of[0], (TOKENS, D), 1.0, 6.0, ((0, 128), (1, 8)))
    expert_ids_keys = jax.random.split(jax.random.fold_in(streams_of[1], 1), TOKENS // TOK)
    expert_ids_turns = jax.random.permutation(jax.random.fold_in(streams_of[1], 3), TOKENS // TOK)
    expert_ids = jax.vmap(lambda own, number: shared_out(jax.random.fold_in(streams_of[1], 2), own, number, TOK, EXPERTS, 2, CAP, 2))(expert_ids_keys, expert_ids_turns).reshape((TOKENS, 2))
    gate_probs = jnp.clip(0.1 + 0.9 * jax.random.uniform(streams_of[2], (TOKENS, 2), jnp.float32) ** block_levels(streams_of[2], (TOKENS, 2), ((0, 128),), -0.2, 0.2), 0.1, 1.0)
    expert_down = centred(streams_of[3], (EXPERTS, EFF, D), D ** -0.5, 0.0625, ((0, 32), (1, 4), (2, 8)))
    saved_gate = centred(streams_of[4], (EXPERTS, SLOTS, EFF), 1.5, 6.0, ((0, 32), (1, 8), (2, 4)))
    saved_up = centred(streams_of[5], (EXPERTS, SLOTS, EFF), 1.5, 6.0, ((0, 32), (1, 8), (2, 4)))
    return dict(out_grad=out_grad, expert_ids=expert_ids, gate_probs=gate_probs, expert_down=expert_down, saved_gate=saved_gate, saved_up=saved_up)


def reference(out_grad, expert_ids, gate_probs, expert_down, saved_gate, saved_up):
    groups = N_DP * N_EXPERT
    entries = TOKENS * 2
    flat_ids = expert_ids.reshape(groups, TOK * 2)
    onehot = (flat_ids[:, :, None] == jnp.arange(EXPERTS, dtype=jnp.int32)[None, None, :]).astype(jnp.int32)
    slot_rank = jnp.sum((jnp.cumsum(onehot, axis=1) - 1) * onehot, axis=2).astype(jnp.int32)
    source = jnp.arange(groups, dtype=jnp.int32)[:, None]
    target = (flat_ids * SLOTS + source * CAP + slot_rank).reshape(-1).astype(jnp.int32)
    owner = jnp.full((EXPERTS * SLOTS,), entries, jnp.int32).at[target].set(jnp.arange(entries, dtype=jnp.int32))
    owner = owner.reshape(EXPERTS, SLOTS)
    gate_flat = jnp.concatenate([gate_probs.reshape(-1), jnp.zeros((1,), jnp.float32)])

    def one_expert(operands):
        owners, weights, pre_gate_raw, pre_up_raw = operands
        valid = owners < entries
        token = jnp.minimum(owners, entries - 1) // 2
        rows = out_grad[token].astype(jnp.float32) * gate_flat[owners][:, None]
        rows = jnp.where(valid[:, None], rows, 0.0).astype(jnp.bfloat16)
        row_blocks = rows.astype(jnp.float32).reshape(SLOTS, N_TENSOR, D // N_TENSOR)
        weight_blocks = weights.astype(jnp.float32).reshape(EFF, N_TENSOR, D // N_TENSOR)
        partial_value = jnp.einsum("std,htd->tsh", row_blocks, weight_blocks)
        partial_value = lax.optimization_barrier(partial_value.astype(jnp.bfloat16)).astype(jnp.float32)
        upstream = jnp.sum(partial_value, axis=0)
        pre_gate = pre_gate_raw.astype(jnp.float32)
        pre_up = pre_up_raw.astype(jnp.float32)
        sigma = jax.nn.sigmoid(pre_gate)
        grad_up = (upstream * pre_gate * sigma).astype(jnp.bfloat16)
        grad_gate = (upstream * pre_up * sigma * (1.0 + pre_gate * (1.0 - sigma))).astype(jnp.bfloat16)
        return grad_gate, grad_up

    grad_gate, grad_up = lax.map(one_expert, (owner, expert_down, saved_gate, saved_up))
    return grad_gate, grad_up
```

```python
import functools

import jax
import jax.numpy as jnp
from jax import lax
from jax.experimental import pallas as pl
from jax.experimental.pallas import tpu as pltpu
from jax.sharding import PartitionSpec as P

MESH = pl.DeviceIdType.MESH
F32 = jnp.float32
BF16 = jnp.bfloat16
AHEAD = 3


def step_residue(s, steps):
    if steps < 4:
        return s
    half = steps // 2
    p = s // 2
    odd = s - 2 * p
    return (1 - odd) * p + odd * ((steps - p) % steps + half * ((half - p) // half))


def row_labels(shape, dim, cap):
    row = lax.broadcasted_iota(jnp.int32, shape, dim)
    core = (row >= 2 * cap).astype(jnp.int32)
    row = row - 2 * cap * core
    expert = (row >= cap).astype(jnp.int32)
    return core, expert, row - cap * expert


def kernel(
    sizes,
    x_ref, meta_ref, w_ref, gate_ref, up_ref,
    out_gate_ref, out_up_ref,
    x_sib, meta_sib, outbox, rows, part, part_in, half_out, half_in, own_sum,
    fac_gate, fac_up, res_gate, res_up,
    sib_send, sib_recv, z_send, z_recv, y_send, y_recv, f_send, f_recv,
    x_send, x_recv, t_send, t_recv,
):
    nz, ny, nx, cap = sizes
    steps = nz // 2
    slab = 4 * cap
    tok, feat = x_ref.shape
    hid = w_ref.shape[1]
    y = lax.axis_index("dp")
    e = lax.axis_index("expert")
    t = lax.axis_index("tensor")
    z, c = e // 2, e % 2
    x, yl = t // 2, t % 2
    right, left = (y + 1) % ny, (y + ny - 1) % ny
    zh, zm = z // steps, z % steps

    def residue(s):
        return (z + step_residue(s, steps)) % steps

    barrier = pltpu.get_barrier_semaphore()

    def greet(device):
        pl.semaphore_signal(barrier, inc=1, device_id=device, device_id_type=MESH)

    greet({"expert": 2 * z + 1 - c})
    greet({"dp": right})
    greet({"dp": left})
    greet({"tensor": 2 * x + 1 - yl})
    for d in range(1, nx):
        greet({"tensor": 2 * ((x + d) % nx) + yl})

    def greet_z(d, carry):
        greet({"expert": 2 * ((z + d) % nz) + c})
        return carry

    lax.fori_loop(1, nz, greet_z, 0)
    pl.semaphore_wait(barrier, 1 + 2 + 1 + (nx - 1) + (nz - 1))

    sib = {"expert": 2 * z + 1 - c}
    copy_meta = pltpu.make_async_remote_copy(
        meta_ref, meta_sib, sib_send.at[0], sib_recv.at[0], device_id=sib, device_id_type=MESH
    )
    copy_x = pltpu.make_async_remote_copy(
        x_ref, x_sib, sib_send.at[1], sib_recv.at[1], device_id=sib, device_id_type=MESH
    )
    copy_meta.start()
    copy_x.start()

    dims = (nz, slab, tok)
    dest = lax.broadcasted_iota(jnp.int32, dims, 0)
    core, expert, rank = row_labels(dims, 1, cap)
    name = (4 * dest + 2 * c + expert).astype(F32)
    earlier = (
        lax.broadcasted_iota(jnp.int32, (tok, tok), 0)
        < lax.broadcasted_iota(jnp.int32, (tok, tok), 1)
    ).astype(F32).astype(BF16)

    def pick(meta, tokens, which):
        mine = core == which
        first = ((name == meta[0:1, :].reshape(1, 1, tok)) & mine).astype(F32)
        second = ((name == meta[1:2, :].reshape(1, 1, tok)) & mine).astype(F32)
        both = first + second
        count = jnp.dot(
            both.reshape(nz * slab, tok).astype(BF16), earlier, preferred_element_type=F32
        ).reshape(dims)
        here = (count == rank.astype(F32)).astype(F32)
        chosen = both * here
        weight = jnp.sum(
            (first * meta[2:3, :].reshape(1, 1, tok) + second * meta[3:4, :].reshape(1, 1, tok))
            * here,
            axis=2, keepdims=True,
        )
        picked = jnp.dot(
            chosen.reshape(nz * slab, tok).astype(BF16), tokens, preferred_element_type=F32
        )
        return picked.reshape(nz, slab, feat), weight

    rows_a, weight_a = pick(meta_ref[...], x_ref[...], c)
    copy_meta.wait_recv()
    copy_x.wait_recv()
    rows_b, weight_b = pick(meta_sib[...], x_sib[...], 1 - c)
    outbox[...] = ((rows_a + rows_b) * (weight_a + weight_b)).astype(BF16)
    rows[y, zm, zh] = outbox[z]

    def z_copy(s, other):
        to = (z - step_residue(s, steps) + nz + other * steps) % nz
        return pltpu.make_async_remote_copy(
            outbox.at[to], rows.at[y, zm, zh], z_send.at[s, other], z_recv.at[s, zh],
            device_id={"expert": 2 * to + c}, device_id_type=MESH,
        )

    def z_wait(s, h):
        pltpu.make_async_remote_copy(
            outbox.at[0], rows.at[y, residue(s), h], z_send.at[s, 0], z_recv.at[s, h],
            device_id=sib, device_id_type=MESH,
        ).wait_recv()

    def z_start(s):
        @pl.when(s > 0)
        def _():
            z_copy(s, 0).start()

        z_copy(s, 1).start()

    def y_copy(s, side):
        to = (right, left)[side]
        return pltpu.make_async_remote_copy(
            rows.at[y, residue(s)], rows.at[y, residue(s)], y_send.at[s, side], y_recv.at[s, side],
            device_id={"dp": to}, device_id_type=MESH,
        )

    def f_copy(s, side):
        source, to = ((left, right), (right, left))[side]
        return pltpu.make_async_remote_copy(
            rows.at[source, residue(s), side], rows.at[source, residue(s), side],
            f_send.at[s, side], f_recv.at[s, side],
            device_id={"dp": to}, device_id_type=MESH,
        )

    def x_copy(s, d):
        to = (x + d) % nx
        return pltpu.make_async_remote_copy(
            part.at[s, to], part_in.at[s, d - 1], x_send.at[s, d - 1], x_recv.at[s, d - 1],
            device_id={"tensor": 2 * to + yl}, device_id_type=MESH,
        )

    def t_copy(s):
        return pltpu.make_async_remote_copy(
            half_out.at[s], half_in.at[s], t_send.at[s], t_recv.at[s],
            device_id={"tensor": 2 * x + 1 - yl}, device_id_type=MESH,
        )

    def spread(s):
        @pl.when(s > 0)
        def _():
            z_wait(s, zh)

        @pl.when(s == 0)
        def _():
            z_wait(s, 1 - zh)

        @pl.when(s > 0)
        def _():
            z_wait(s, 1 - zh)

        y_copy(s, 0).start()
        y_copy(s, 1).start()

    def forward(s):
        y_copy(s, 0).wait_recv()
        f_copy(s, 0).start()
        y_copy(s, 1).wait_recv()
        f_copy(s, 1).start()

    def multiply(s):
        f_copy(s, 0).wait_recv()
        f_copy(s, 1).wait_recv()
        m = residue(s)
        block = jnp.concatenate(
            [rows[i, m].astype(F32).reshape(2 * slab, feat) for i in range(ny)], axis=0
        ).astype(BF16)
        contract = (((1,), (1,)), ((), ()))
        a = lax.dot_general(block, w_ref[0], contract, preferred_element_type=F32)
        b = lax.dot_general(block, w_ref[1], contract, preferred_element_type=F32)
        _, which, _ = row_labels((2 * ny, slab, hid), 1, cap)
        value = jnp.where(
            which == 1, b.reshape(2 * ny, slab, hid), a.reshape(2 * ny, slab, hid)
        )
        part[s] = value.astype(BF16).reshape(ny, 2, slab, hid)
        for d in range(1, nx):
            x_copy(s, d).start()

    def reduce(s):
        for d in range(1, nx):
            x_copy(s, d).wait_recv()

        def total(h):
            value = part[s, x, h].astype(F32)
            for d in range(nx - 1):
                value = value + part_in[s, d, h].astype(F32)
            return value

        half_out[s] = total(1 - yl).astype(BF16)
        t_copy(s).start()
        own_sum[s] = total(yl)

    def finish(s):
        t_copy(s).wait_recv()
        upstream = own_sum[s] + half_in[s].astype(F32)
        res_gate[s] = upstream * fac_gate[s]
        res_up[s] = upstream * fac_up[s]

    for s in range(min(AHEAD, steps)):
        z_start(jnp.int32(s))

    col = lax.broadcasted_iota(jnp.int32, (slab, 2 * steps * 2 * cap), 1)
    core2, expert2, rank2 = row_labels(col.shape, 0, cap)
    base = expert2 * (steps * 2 * cap) + core2 * cap + rank2
    order = jnp.concatenate(
        [(col == base + 2 * cap * residue(s)).astype(F32) for s in range(steps)], axis=0
    ).astype(BF16)

    def to_slabs(ref):
        return jnp.dot(order, ref[...], preferred_element_type=F32).reshape(steps, slab, hid)

    pre_gate = to_slabs(gate_ref)
    pre_up = to_slabs(up_ref)
    sigma = jax.nn.sigmoid(pre_gate)
    fac_up[...] = pre_gate * sigma
    fac_gate[...] = pre_up * sigma * (1.0 + pre_gate * (1.0 - sigma))

    def step(s, carry):
        @pl.when(s + AHEAD < steps)
        def _():
            z_start(s + AHEAD)

        def stage(lag, body):
            @pl.when((s >= lag) & (s < steps + lag))
            def _():
                body(s - lag)

        stage(0, spread)
        stage(1, forward)
        stage(3, multiply)
        stage(4, reduce)
        stage(5, finish)
        return carry

    lax.fori_loop(0, steps + 5, step, 0)

    def from_slabs(ref):
        value = ref[...].reshape(steps * slab, hid).astype(BF16)
        return lax.dot_general(
            order, value, (((0,), (0,)), ((), ())), preferred_element_type=F32
        ).astype(BF16)

    out_gate_ref[...] = from_slabs(res_gate)
    out_up_ref[...] = from_slabs(res_up)

    copy_meta.wait_send()
    copy_x.wait_send()

    def drain(s, carry):
        @pl.when(s > 0)
        def _():
            z_copy(s, 0).wait_send()

        z_copy(s, 1).wait_send()
        for side in range(2):
            y_copy(s, side).wait_send()
            f_copy(s, side).wait_send()
        for d in range(1, nx):
            x_copy(s, d).wait_send()
        t_copy(s).wait_send()
        return carry

    lax.fori_loop(0, steps, drain, 0)


def shards(out_grad, expert_ids, gate_probs, expert_down, saved_gate, saved_up):
    tok, feat = out_grad.shape
    hid = expert_down.shape[1]
    nz = lax.axis_size("expert") // 2
    ny = lax.axis_size("dp")
    nx = lax.axis_size("tensor") // 2
    cap = saved_gate.shape[1] * 2 * nx // (2 * nz * ny)
    steps, slab = nz // 2, 4 * cap
    assert nx == ny and expert_down.shape[0] == 2
    meta = jnp.concatenate(
        [expert_ids.T.astype(F32), gate_probs.T, jnp.zeros((4, tok), F32)], axis=0
    )
    dma = pltpu.SemaphoreType.DMA
    out_rows = 2 * saved_gate.shape[1]
    out = jax.ShapeDtypeStruct((out_rows, hid), BF16)
    vmem = pl.BlockSpec(memory_space=pltpu.VMEM)
    grad_gate, grad_up = pl.pallas_call(
        functools.partial(kernel, (nz, ny, nx, cap)),
        out_shape=(out, out),
        in_specs=[vmem] * 5,
        out_specs=(vmem, vmem),
        scratch_shapes=[
            pltpu.VMEM((tok, feat), BF16),
            pltpu.VMEM((8, tok), F32),
            pltpu.VMEM((nz, slab, feat), BF16),
            pltpu.VMEM((ny, steps, 2, slab, feat), BF16),
            pltpu.VMEM((steps, ny, 2, slab, hid), BF16),
            pltpu.VMEM((steps, nx - 1, 2, slab, hid), BF16),
            pltpu.VMEM((steps, slab, hid), BF16),
            pltpu.VMEM((steps, slab, hid), BF16),
            pltpu.VMEM((steps, slab, hid), F32),
            pltpu.VMEM((steps, slab, hid), F32),
            pltpu.VMEM((steps, slab, hid), F32),
            pltpu.VMEM((steps, slab, hid), F32),
            pltpu.VMEM((steps, slab, hid), F32),
            dma((2,)), dma((2,)),
            dma((steps, 2)), dma((steps, 2)),
            dma((steps, 2)), dma((steps, 2)),
            dma((steps, 2)), dma((steps, 2)),
            dma((steps, nx - 1)), dma((steps, nx - 1)),
            dma((steps,)), dma((steps,)),
        ],
        compiler_params=pltpu.CompilerParams(
            collective_id=0, has_side_effects=True, vmem_limit_bytes=48 * 1024 * 1024
        ),
    )(
        out_grad, meta, expert_down,
        saved_gate.reshape(out_rows, hid), saved_up.reshape(out_rows, hid),
    )
    return grad_gate.reshape(saved_gate.shape), grad_up.reshape(saved_up.shape)


def solution(mesh):
    in_specs = (
        P(("dp", "expert"), "tensor"),
        P(("dp", "expert"), None),
        P(("dp", "expert"), None),
        P("expert", "dp", "tensor"),
        P("expert", "tensor", "dp"),
        P("expert", "tensor", "dp"),
    )
    out_specs = (P("expert", "tensor", "dp"), P("expert", "tensor", "dp"))
    return jax.shard_map(shards, mesh=mesh, in_specs=in_specs, out_specs=out_specs, check_vma=False)
```

```python
import functools

import jax
import jax.numpy as jnp
from jax import lax
from jax.experimental import pallas as pl
from jax.experimental.pallas import tpu as pltpu
from jax.sharding import PartitionSpec as P

MESH = pl.DeviceIdType.MESH
F32 = jnp.float32
BF16 = jnp.bfloat16
AHEAD = 3
FORWARD, MULTIPLY, REDUCE, FINISH = 2, 4, 6, 7


def row_labels(shape, dim, cap):
    row = lax.broadcasted_iota(jnp.int32, shape, dim)
    core = (row >= 2 * cap).astype(jnp.int32)
    row = row - 2 * cap * core
    expert = (row >= cap).astype(jnp.int32)
    return core, expert, row - cap * expert


def kernel(
    sizes,
    x_ref, ids_ref, prob_ref, w_ref, gate_ref, up_ref,
    out_gate_ref, out_up_ref,
    x_both, ids_both, prob_both, w, gate, up,
    outbox, rows, part, part_in, half_out, half_in, own_sum,
    fac_gate, fac_up, res_gate, res_up,
    load, sib_send, sib_recv, z_send, z_recv, y_send, y_recv, f_send, f_recv,
    x_send, x_recv, t_send, t_recv,
):
    nz, ny, nx, cap = sizes
    steps = nz // 2
    slab = 4 * cap
    tok, feat = x_ref.shape
    hid = w_ref.shape[1]
    y = lax.axis_index("dp")
    e = lax.axis_index("expert")
    t = lax.axis_index("tensor")
    z, c = e // 2, e % 2
    x, yl = t // 2, t % 2
    right, left = (y + 1) % ny, (y + ny - 1) % ny
    sib = {"expert": 2 * z + 1 - c}
    pair = {"tensor": 2 * x + 1 - yl}

    barrier = pltpu.get_barrier_semaphore()

    def greet(device):
        pl.semaphore_signal(barrier, inc=1, device_id=device, device_id_type=MESH)

    greet(sib)
    greet({"dp": right})
    greet({"dp": left})
    greet(pair)
    for d in range(1, nx):
        greet({"tensor": 2 * ((x + d) % nx) + yl})

    def greet_z(d, carry):
        greet({"expert": 2 * ((z + d) % nz) + c})
        return carry

    lax.fori_loop(1, nz, greet_z, 0)

    loads = [
        pltpu.make_async_copy(source, to, load.at[i])
        for i, (source, to) in enumerate(
            [
                (ids_ref, ids_both.at[0]), (prob_ref, prob_both.at[0]), (x_ref, x_both.at[0]),
                (w_ref, w), (gate_ref, gate), (up_ref, up),
            ]
        )
    ]
    for copy in loads:
        copy.start()

    dims = (nz, slab, tok)
    dest = lax.broadcasted_iota(jnp.int32, dims, 0)
    core, expert, rank = row_labels(dims, 1, cap)
    name = 4 * dest + 2 * c + expert
    earlier = (
        lax.broadcasted_iota(jnp.int32, (tok, tok), 0)
        < lax.broadcasted_iota(jnp.int32, (tok, tok), 1)
    ).astype(F32).astype(BF16)

    def pick(i, which):
        mine = core == which
        first = ((name == ids_both[i, 0:1, :].reshape(1, 1, tok)) & mine).astype(F32)
        second = ((name == ids_both[i, 1:2, :].reshape(1, 1, tok)) & mine).astype(F32)
        both = first + second
        count = jnp.dot(
            both.reshape(nz * slab, tok).astype(BF16), earlier, preferred_element_type=F32
        ).reshape(dims)
        here = (count == rank.astype(F32)).astype(F32)
        weight = (
            first * prob_both[i, 0:1, :].reshape(1, 1, tok)
            + second * prob_both[i, 1:2, :].reshape(1, 1, tok)
        ) * here
        return (both * here).reshape(nz * slab, tok).astype(BF16), weight

    loads[0].wait()
    loads[1].wait()
    chosen_a, weight_a = pick(0, c)

    pl.semaphore_wait(barrier, 1 + 2 + 1 + (nx - 1) + (nz - 1))

    exchange = [
        pltpu.make_async_remote_copy(
            source, to, sib_send.at[i], sib_recv.at[i], device_id=sib, device_id_type=MESH
        )
        for i, (source, to) in enumerate(
            [(ids_ref, ids_both.at[1]), (prob_ref, prob_both.at[1]), (x_ref, x_both.at[1])]
        )
    ]
    for copy in exchange:
        copy.start()
    exchange[0].wait_recv()
    exchange[1].wait_recv()
    chosen_b, weight_b = pick(1, 1 - c)
    weight = jnp.sum(weight_a + weight_b, axis=2, keepdims=True)
    loads[2].wait()
    exchange[2].wait_recv()
    picked = jnp.dot(
        jnp.concatenate([chosen_a, chosen_b], axis=1), x_both[...].reshape(2 * tok, feat),
        preferred_element_type=F32,
    )
    outbox[...] = (picked.reshape(nz, slab, feat) * weight).astype(BF16)

    def z_copy(s, j):
        to = (z + s, z + nz - s - 1)[j] % nz
        return pltpu.make_async_remote_copy(
            outbox.at[to], rows.at[y, s, j], z_send.at[s, j], z_recv.at[s, j],
            device_id={"expert": 2 * to + c}, device_id_type=MESH,
        )

    def z_start(s):
        @pl.when(s > 0)
        def _():
            z_copy(s, 0).start()

        z_copy(s, 1).start()

    def y_copy(s, j, side):
        return pltpu.make_async_remote_copy(
            rows.at[y, s, j], rows.at[y, s, j], y_send.at[s, j, side], y_recv.at[s, j, side],
            device_id={"dp": (right, left)[side]}, device_id_type=MESH,
        )

    def f_copy(s, j):
        source, to = ((left, right), (right, left))[j]
        return pltpu.make_async_remote_copy(
            rows.at[source, s, j], rows.at[source, s, j], f_send.at[s, j], f_recv.at[s, j],
            device_id={"dp": to}, device_id_type=MESH,
        )

    def x_copy(s, d):
        to = (x + d) % nx
        return pltpu.make_async_remote_copy(
            part.at[s, to], part_in.at[s, d - 1], x_send.at[s, d - 1], x_recv.at[s, d - 1],
            device_id={"tensor": 2 * to + yl}, device_id_type=MESH,
        )

    def t_copy(m):
        return pltpu.make_async_remote_copy(
            half_out.at[m], half_in.at[m], t_send.at[m], t_recv.at[m],
            device_id=pair, device_id_type=MESH,
        )

    def place(s, j):
        at = (z + nz - s, z + s + 1)[j] % nz
        return at // steps, at % steps

    def spread(s):
        @pl.when(s > 0)
        def _():
            z_copy(s, 0).wait_recv()

        for j in range(2):
            if j == 1:
                z_copy(s, 1).wait_recv()
            for side in range(2):
                y_copy(s, j, side).start()

    def forward(s):
        for j in range(2):
            y_copy(s, j, j).wait_recv()
            f_copy(s, j).start()

    def multiply(s):
        for j in range(2):
            y_copy(s, j, 1 - j).wait_recv()
        for j in range(2):
            f_copy(s, j).wait_recv()
        block = jnp.concatenate(
            [rows[i, s].astype(F32).reshape(2 * slab, feat) for i in range(ny)], axis=0
        ).astype(BF16)
        contract = (((1,), (1,)), ((), ()))
        a = lax.dot_general(block, w[0], contract, preferred_element_type=F32)
        b = lax.dot_general(block, w[1], contract, preferred_element_type=F32)
        _, which, _ = row_labels((2 * ny, slab, hid), 1, cap)
        value = jnp.where(
            which == 1, b.reshape(2 * ny, slab, hid), a.reshape(2 * ny, slab, hid)
        )
        part[s] = value.astype(BF16).reshape(ny, 2, slab, hid)
        for d in range(1, nx):
            x_copy(s, d).start()

    def reduce(s):
        for d in range(1, nx):
            x_copy(s, d).wait_recv()
        for j in range(2):
            half, m = place(s, j)
            value = part[s, x, j].astype(F32)
            for d in range(nx - 1):
                value = value + part_in[s, d, j].astype(F32)

            @pl.when(half == yl)
            def _():
                own_sum[m] = value

            @pl.when(half != yl)
            def _():
                half_out[m] = value.astype(BF16)
                t_copy(m).start()

    def finish(s):
        for j in range(2):
            half, m = place(s, j)

            @pl.when(half == yl)
            def _():
                t_copy(m).wait_recv()
                upstream = own_sum[m] + half_in[m].astype(F32)
                res_gate[m] = upstream * fac_gate[m]
                res_up[m] = upstream * fac_up[m]

    rows[y, 0, 0] = outbox[z]
    for s in range(min(AHEAD, steps)):
        z_start(jnp.int32(s))

    col = lax.broadcasted_iota(jnp.int32, (slab, 2 * steps * 2 * cap), 1)
    core2, expert2, rank2 = row_labels(col.shape, 0, cap)
    base = expert2 * (steps * 2 * cap) + core2 * cap + rank2
    order = jnp.concatenate(
        [(col == base + 2 * cap * m).astype(F32) for m in range(steps)], axis=0
    ).astype(BF16)

    def factors():
        def to_slabs(ref):
            return jnp.dot(order, ref[...], preferred_element_type=F32).reshape(steps, slab, hid)

        for copy in loads[3:]:
            copy.wait()
        pre_gate = to_slabs(gate)
        pre_up = to_slabs(up)
        sigma = jax.nn.sigmoid(pre_gate)
        fac_up[...] = pre_gate * sigma
        fac_gate[...] = pre_up * sigma * (1.0 + pre_gate * (1.0 - sigma))

    def step(s, carry):
        @pl.when(s + AHEAD < steps)
        def _():
            z_start(s + AHEAD)

        def stage(lag, body):
            @pl.when((s >= lag) & (s < steps + lag))
            def _():
                body(s - lag)

        stage(0, spread)
        stage(FORWARD, forward)

        @pl.when(s == 1)
        def _():
            factors()

        stage(MULTIPLY, multiply)
        stage(REDUCE, reduce)
        stage(FINISH, finish)
        return carry

    lax.fori_loop(0, steps + FINISH, step, 0)

    def from_slabs(ref):
        value = ref[...].reshape(steps * slab, hid).astype(BF16)
        return lax.dot_general(
            order, value, (((0,), (0,)), ((), ())), preferred_element_type=F32
        ).astype(BF16)

    out_gate_ref[...] = from_slabs(res_gate)
    out_up_ref[...] = from_slabs(res_up)

    for copy in exchange:
        copy.wait_send()

    def drain(s, carry):
        @pl.when(s > 0)
        def _():
            z_copy(s, 0).wait_send()

        z_copy(s, 1).wait_send()
        for j in range(2):
            for side in range(2):
                y_copy(s, j, side).wait_send()
            f_copy(s, j).wait_send()
            half, m = place(s, j)

            @pl.when(half != yl)
            def _():
                t_copy(m).wait_send()

        for d in range(1, nx):
            x_copy(s, d).wait_send()
        return carry

    lax.fori_loop(0, steps, drain, 0)


def shards(out_grad, expert_ids, gate_probs, expert_down, saved_gate, saved_up):
    tok, feat = out_grad.shape
    hid = expert_down.shape[1]
    nz = lax.axis_size("expert") // 2
    ny = lax.axis_size("dp")
    nx = lax.axis_size("tensor") // 2
    cap = saved_gate.shape[1] * 2 * nx // (2 * nz * ny)
    steps, slab = nz // 2, 4 * cap
    assert nx == ny and expert_down.shape[0] == 2
    dma = pltpu.SemaphoreType.DMA
    out_rows = 2 * saved_gate.shape[1]
    out = jax.ShapeDtypeStruct((out_rows, hid), BF16)
    vmem = pl.BlockSpec(memory_space=pltpu.VMEM)
    hbm = pl.BlockSpec(memory_space=pl.ANY)
    grad_gate, grad_up = pl.pallas_call(
        functools.partial(kernel, (nz, ny, nx, cap)),
        out_shape=(out, out),
        in_specs=[hbm] * 6,
        out_specs=(vmem, vmem),
        scratch_shapes=[
            pltpu.VMEM((2, tok, feat), BF16),
            pltpu.VMEM((2, 2, tok), jnp.int32),
            pltpu.VMEM((2, 2, tok), F32),
            pltpu.VMEM((2, hid, feat), BF16),
            pltpu.VMEM((out_rows, hid), BF16),
            pltpu.VMEM((out_rows, hid), BF16),
            pltpu.VMEM((nz, slab, feat), BF16),
            pltpu.VMEM((ny, steps, 2, slab, feat), BF16),
            pltpu.VMEM((steps, ny, 2, slab, hid), BF16),
            pltpu.VMEM((steps, nx - 1, 2, slab, hid), BF16),
            pltpu.VMEM((steps, slab, hid), BF16),
            pltpu.VMEM((steps, slab, hid), BF16),
            pltpu.VMEM((steps, slab, hid), F32),
            pltpu.VMEM((steps, slab, hid), F32),
            pltpu.VMEM((steps, slab, hid), F32),
            pltpu.VMEM((steps, slab, hid), F32),
            pltpu.VMEM((steps, slab, hid), F32),
            dma((6,)), dma((3,)), dma((3,)),
            dma((steps, 2)), dma((steps, 2)),
            dma((steps, 2, 2)), dma((steps, 2, 2)),
            dma((steps, 2)), dma((steps, 2)),
            dma((steps, nx - 1)), dma((steps, nx - 1)),
            dma((steps,)), dma((steps,)),
        ],
        compiler_params=pltpu.CompilerParams(
            collective_id=0, has_side_effects=True, vmem_limit_bytes=60 * 1024 * 1024
        ),
    )(
        out_grad, expert_ids.T, gate_probs.T, expert_down,
        saved_gate.reshape(out_rows, hid), saved_up.reshape(out_rows, hid),
    )
    return grad_gate.reshape(saved_gate.shape), grad_up.reshape(saved_up.shape)


def solution(mesh):
    in_specs = (
        P(("dp", "expert"), "tensor"),
        P(("dp", "expert"), None),
        P(("dp", "expert"), None),
        P("expert", "dp", "tensor"),
        P("expert", "tensor", "dp"),
        P("expert", "tensor", "dp"),
    )
    out_specs = (P("expert", "tensor", "dp"), P("expert", "tensor", "dp"))
    return jax.shard_map(shards, mesh=mesh, in_specs=in_specs, out_specs=out_specs, check_vma=False)
```

```python
import functools

import jax
import jax.numpy as jnp
from jax import lax
from jax.experimental import pallas as pl
from jax.experimental.pallas import tpu as pltpu
from jax.sharding import PartitionSpec as P

MESH = pl.DeviceIdType.MESH
F32 = jnp.float32
BF16 = jnp.bfloat16
AHEAD = 4
FORWARD, MULTIPLY, REDUCE, FINISH = 2, 4, 7, 9


def row_labels(shape, dim, cap):
    row = lax.broadcasted_iota(jnp.int32, shape, dim)
    core = (row >= 2 * cap).astype(jnp.int32)
    row = row - 2 * cap * core
    expert = (row >= cap).astype(jnp.int32)
    return core, expert, row - cap * expert


def kernel(
    sizes,
    x_ref, ids_ref, prob_ref, w_ref, gate_ref, up_ref,
    out_gate_ref, out_up_ref,
    x_both, ids_both, prob_both, w, gate, up,
    outbox, rows, part, part_in, half_out, half_in, own_sum,
    fac_gate, fac_up, res_gate, res_up,
    load, sib_send, sib_recv, z_send, z_recv, y_send, y_recv, f_send, f_recv,
    x_send, x_recv, t_send, t_recv, ready,
):
    nz, ny, nx, cap = sizes
    steps = nz // 2
    slab = 4 * cap
    tok, feat = x_ref.shape
    hid = w_ref.shape[1]
    y = lax.axis_index("dp")
    e = lax.axis_index("expert")
    t = lax.axis_index("tensor")
    z, c = e // 2, e % 2
    x, yl = t // 2, t % 2
    right, left = (y + 1) % ny, (y + ny - 1) % ny
    sib = {"expert": 2 * z + 1 - c}
    pair = {"tensor": 2 * x + 1 - yl}

    barrier = pltpu.get_barrier_semaphore()

    def greet(device):
        pl.semaphore_signal(barrier, inc=1, device_id=device, device_id_type=MESH)

    greet(sib)
    greet({"dp": right})
    greet({"dp": left})
    greet(pair)
    for d in range(1, nx):
        greet({"tensor": 2 * ((x + d) % nx) + yl})

    def greet_above(i, carry):
        greet({"expert": 2 * i + c})
        return carry

    lax.fori_loop(z + 1, nz, greet_above, 0)

    loads = [
        pltpu.make_async_copy(source, to, load.at[i])
        for i, (source, to) in enumerate(
            [
                (ids_ref, ids_both.at[0]), (prob_ref, prob_both.at[0]), (x_ref, x_both.at[0]),
                (w_ref, w), (gate_ref, gate), (up_ref, up),
            ]
        )
    ]
    for copy in loads:
        copy.start()

    dims = (nz, slab, tok)
    dest = lax.broadcasted_iota(jnp.int32, dims, 0)
    core, expert, rank = row_labels(dims, 1, cap)
    name = 4 * dest + 2 * c + expert
    earlier = (
        lax.broadcasted_iota(jnp.int32, (tok, tok), 0)
        < lax.broadcasted_iota(jnp.int32, (tok, tok), 1)
    ).astype(F32).astype(BF16)

    def pick(i, which):
        mine = core == which
        first = ((name == ids_both[i, 0:1, :].reshape(1, 1, tok)) & mine).astype(F32)
        second = ((name == ids_both[i, 1:2, :].reshape(1, 1, tok)) & mine).astype(F32)
        both = first + second
        count = jnp.dot(
            both.reshape(nz * slab, tok).astype(BF16), earlier, preferred_element_type=F32
        ).reshape(dims)
        here = (count == rank.astype(F32)).astype(F32)
        weight = (
            first * prob_both[i, 0:1, :].reshape(1, 1, tok)
            + second * prob_both[i, 1:2, :].reshape(1, 1, tok)
        ) * here
        return (both * here).reshape(nz * slab, tok).astype(BF16), weight

    loads[0].wait()
    loads[1].wait()
    chosen_a, weight_a = pick(0, c)

    pl.semaphore_wait(barrier, 1 + 2 + 1 + (nx - 1) + z)

    exchange = [
        pltpu.make_async_remote_copy(
            source, to, sib_send.at[i], sib_recv.at[i], device_id=sib, device_id_type=MESH
        )
        for i, (source, to) in enumerate(
            [(ids_ref, ids_both.at[1]), (prob_ref, prob_both.at[1]), (x_ref, x_both.at[1])]
        )
    ]
    for copy in exchange:
        copy.start()

    def answer_below(i, carry):
        pl.semaphore_signal(
            ready.at[z], inc=1, device_id={"expert": 2 * i + c}, device_id_type=MESH
        )
        return carry

    lax.fori_loop(0, z, answer_below, 0)
    exchange[0].wait_recv()
    exchange[1].wait_recv()
    chosen_b, weight_b = pick(1, 1 - c)
    weight = jnp.sum(weight_a + weight_b, axis=2, keepdims=True)
    loads[2].wait()
    exchange[2].wait_recv()
    picked = jnp.dot(
        jnp.concatenate([chosen_a, chosen_b], axis=1), x_both[...].reshape(2 * tok, feat),
        preferred_element_type=F32,
    )
    outbox[...] = (picked.reshape(nz, slab, feat) * weight).astype(BF16)

    def z_to(s, j):
        return (z + s, z + nz - s - 1)[j] % nz

    def z_copy(s, j):
        to = z_to(s, j)
        return pltpu.make_async_remote_copy(
            outbox.at[to], rows.at[y, s, j], z_send.at[s, j], z_recv.at[s, j],
            device_id={"expert": 2 * to + c}, device_id_type=MESH,
        )

    def z_start(s, j):
        to = z_to(s, j)

        @pl.when(to > z)
        def _():
            pl.semaphore_wait(ready.at[to], 1)

        z_copy(s, j).start()

    def y_copy(s, j, side):
        return pltpu.make_async_remote_copy(
            rows.at[y, s, j], rows.at[y, s, j], y_send.at[s, j, side], y_recv.at[s, j, side],
            device_id={"dp": (y + 1 + side * (ny - 2)) % ny}, device_id_type=MESH,
        )

    def f_copy(s, j):
        source, to = ((left, right), (right, left))[j]
        return pltpu.make_async_remote_copy(
            rows.at[source, s, j], rows.at[source, s, j], f_send.at[s, j], f_recv.at[s, j],
            device_id={"dp": to}, device_id_type=MESH,
        )

    def x_copy(s, d):
        to = (x + d) % nx
        return pltpu.make_async_remote_copy(
            part.at[s, to], part_in.at[s, d - 1], x_send.at[s, d - 1], x_recv.at[s, d - 1],
            device_id={"tensor": 2 * to + yl}, device_id_type=MESH,
        )

    def t_copy(m):
        return pltpu.make_async_remote_copy(
            half_out.at[m], half_in.at[m], t_send.at[m], t_recv.at[m],
            device_id=pair, device_id_type=MESH,
        )

    def place(s, j):
        at = (z + nz - s, z + s + 1)[j] % nz
        return at // steps, at % steps

    def spread(s):
        @pl.when(s > 0)
        def _():
            z_copy(s, 0).wait_recv()
            for side in (c, 1 - c):
                y_copy(s, 0, side).start()

        z_copy(s, 1).wait_recv()
        for side in (c, 1 - c):
            y_copy(s, 1, side).start()

    def forward(s):
        for j in range(2):
            y_copy(s, j, j).wait_recv()
            f_copy(s, j).start()

    def multiply(s):
        for j in range(2):
            y_copy(s, j, 1 - j).wait_recv()
        for j in range(2):
            f_copy(s, j).wait_recv()
        block = jnp.concatenate(
            [rows[i, s].astype(F32).reshape(2 * slab, feat) for i in range(ny)], axis=0
        ).astype(BF16)
        contract = (((1,), (1,)), ((), ()))
        a = lax.dot_general(block, w[0], contract, preferred_element_type=F32)
        b = lax.dot_general(block, w[1], contract, preferred_element_type=F32)
        _, which, _ = row_labels((2 * ny, slab, hid), 1, cap)
        value = jnp.where(
            which == 1, b.reshape(2 * ny, slab, hid), a.reshape(2 * ny, slab, hid)
        )
        part[s] = value.astype(BF16).reshape(ny, 2, slab, hid)
        for i in (2, 1, 3):
            x_copy(s, i + c * (nx - 2 * i)).start()

    def reduce(s):
        for d in range(1, nx):
            x_copy(s, d).wait_recv()
        for j in range(2):
            half, m = place(s, j)
            value = part[s, x, j].astype(F32)
            for d in range(nx - 1):
                value = value + part_in[s, d, j].astype(F32)

            @pl.when(half == yl)
            def _():
                own_sum[m] = value

            @pl.when(half != yl)
            def _():
                half_out[m] = value.astype(BF16)
                t_copy(m).start()

    def finish(s):
        for j in range(2):
            half, m = place(s, j)

            @pl.when(half == yl)
            def _():
                t_copy(m).wait_recv()
                upstream = own_sum[m] + half_in[m].astype(F32)
                res_gate[m] = upstream * fac_gate[m]
                res_up[m] = upstream * fac_up[m]

    def drain(s):
        @pl.when(s > 0)
        def _():
            z_copy(s, 0).wait_send()

        z_copy(s, 1).wait_send()
        for j in range(2):
            for side in range(2):
                y_copy(s, j, side).wait_send()
            f_copy(s, j).wait_send()
            half, m = place(s, j)

            @pl.when(half != yl)
            def _():
                t_copy(m).wait_send()

        for d in range(1, nx):
            x_copy(s, d).wait_send()

    rows[y, 0, 0] = outbox[z]
    for side in (c, 1 - c):
        y_copy(0, 0, side).start()
    for s in range(1, min(AHEAD, steps)):
        z_start(jnp.int32(s), 0)
    for s in range(min(AHEAD, steps)):
        z_start(jnp.int32(s), 1)

    col = lax.broadcasted_iota(jnp.int32, (slab, 2 * steps * 2 * cap), 1)
    core2, expert2, rank2 = row_labels(col.shape, 0, cap)
    base = expert2 * (steps * 2 * cap) + core2 * cap + rank2
    order = jnp.concatenate(
        [(col == base + 2 * cap * m).astype(F32) for m in range(steps)], axis=0
    ).astype(BF16)

    def factors():
        def to_slabs(ref):
            return jnp.dot(order, ref[...], preferred_element_type=F32).reshape(steps, slab, hid)

        for copy in loads[3:]:
            copy.wait()
        pre_gate = to_slabs(gate)
        pre_up = to_slabs(up)
        sigma = jax.nn.sigmoid(pre_gate)
        fac_up[...] = pre_gate * sigma
        fac_gate[...] = pre_up * sigma * (1.0 + pre_gate * (1.0 - sigma))

    def step(s, carry):
        @pl.when(s + AHEAD < steps)
        def _():
            z_start(s + AHEAD, 0)
            z_start(s + AHEAD, 1)

        def stage(lag, body):
            @pl.when((s >= lag) & (s < steps + lag))
            def _():
                body(s - lag)

        stage(0, spread)
        stage(FORWARD, forward)

        @pl.when(s == 1)
        def _():
            factors()

        stage(MULTIPLY, multiply)
        stage(REDUCE, reduce)
        stage(FINISH, finish)
        stage(FINISH, drain)
        return carry

    lax.fori_loop(0, steps + FINISH, step, 0)

    def from_slabs(ref):
        value = ref[...].reshape(steps * slab, hid).astype(BF16)
        return lax.dot_general(
            order, value, (((0,), (0,)), ((), ())), preferred_element_type=F32
        ).astype(BF16)

    out_gate_ref[...] = from_slabs(res_gate)
    out_up_ref[...] = from_slabs(res_up)

    for copy in exchange:
        copy.wait_send()


def shards(out_grad, expert_ids, gate_probs, expert_down, saved_gate, saved_up):
    tok, feat = out_grad.shape
    hid = expert_down.shape[1]
    nz = lax.axis_size("expert") // 2
    ny = lax.axis_size("dp")
    nx = lax.axis_size("tensor") // 2
    cap = saved_gate.shape[1] * 2 * nx // (2 * nz * ny)
    steps, slab = nz // 2, 4 * cap
    assert nx == ny and expert_down.shape[0] == 2
    dma = pltpu.SemaphoreType.DMA
    out_rows = 2 * saved_gate.shape[1]
    out = jax.ShapeDtypeStruct((out_rows, hid), BF16)
    vmem = pl.BlockSpec(memory_space=pltpu.VMEM)
    hbm = pl.BlockSpec(memory_space=pl.ANY)
    grad_gate, grad_up = pl.pallas_call(
        functools.partial(kernel, (nz, ny, nx, cap)),
        out_shape=(out, out),
        in_specs=[hbm] * 6,
        out_specs=(vmem, vmem),
        scratch_shapes=[
            pltpu.VMEM((2, tok, feat), BF16),
            pltpu.VMEM((2, 2, tok), jnp.int32),
            pltpu.VMEM((2, 2, tok), F32),
            pltpu.VMEM((2, hid, feat), BF16),
            pltpu.VMEM((out_rows, hid), BF16),
            pltpu.VMEM((out_rows, hid), BF16),
            pltpu.VMEM((nz, slab, feat), BF16),
            pltpu.VMEM((ny, steps, 2, slab, feat), BF16),
            pltpu.VMEM((steps, ny, 2, slab, hid), BF16),
            pltpu.VMEM((steps, nx - 1, 2, slab, hid), BF16),
            pltpu.VMEM((steps, slab, hid), BF16),
            pltpu.VMEM((steps, slab, hid), BF16),
            pltpu.VMEM((steps, slab, hid), F32),
            pltpu.VMEM((steps, slab, hid), F32),
            pltpu.VMEM((steps, slab, hid), F32),
            pltpu.VMEM((steps, slab, hid), F32),
            pltpu.VMEM((steps, slab, hid), F32),
            dma((6,)), dma((3,)), dma((3,)),
            dma((steps, 2)), dma((steps, 2)),
            dma((steps, 2, 2)), dma((steps, 2, 2)),
            dma((steps, 2)), dma((steps, 2)),
            dma((steps, nx - 1)), dma((steps, nx - 1)),
            dma((steps,)), dma((steps,)), pltpu.SemaphoreType.REGULAR((nz,)),
        ],
        compiler_params=pltpu.CompilerParams(
            collective_id=0, has_side_effects=True, vmem_limit_bytes=60 * 1024 * 1024
        ),
    )(
        out_grad, expert_ids.T, gate_probs.T, expert_down,
        saved_gate.reshape(out_rows, hid), saved_up.reshape(out_rows, hid),
    )
    return grad_gate.reshape(saved_gate.shape), grad_up.reshape(saved_up.shape)


def solution(mesh):
    in_specs = (
        P(("dp", "expert"), "tensor"),
        P(("dp", "expert"), None),
        P(("dp", "expert"), None),
        P("expert", "dp", "tensor"),
        P("expert", "tensor", "dp"),
        P("expert", "tensor", "dp"),
    )
    out_specs = (P("expert", "tensor", "dp"), P("expert", "tensor", "dp"))
    return jax.shard_map(shards, mesh=mesh, in_specs=in_specs, out_specs=out_specs, check_vma=False)
```

```python
import functools

import jax
import jax.numpy as jnp
from jax import lax
from jax.experimental import pallas as pl
from jax.experimental.pallas import tpu as pltpu
from jax.sharding import PartitionSpec as P

MESH = pl.DeviceIdType.MESH
F32 = jnp.float32
BF16 = jnp.bfloat16
AHEAD = 4
FORWARD, MULTIPLY, REDUCE, FINISH = 2, 4, 7, 9


def row_labels(shape, dim, cap):
    row = lax.broadcasted_iota(jnp.int32, shape, dim)
    core = (row >= 2 * cap).astype(jnp.int32)
    row = row - 2 * cap * core
    expert = (row >= cap).astype(jnp.int32)
    return core, expert, row - cap * expert


def kernel(
    sizes,
    x_ref, ids_ref, prob_ref, w_ref, gate_ref, up_ref,
    out_gate_ref, out_up_ref,
    x_both, ids_both, prob_both, w, gate, up,
    outbox, rows, part, part_in, half_out, half_in, own_sum,
    fac_gate, fac_up, res_gate, res_up,
    load, sib_send, sib_recv, z_send, z_recv, y_send, y_recv, f_send, f_recv,
    x_send, x_recv, t_send, t_recv, ready,
):
    nz, ny, nx, cap = sizes
    steps = nz // 2
    slab = 4 * cap
    tok, feat = x_ref.shape
    hid = w_ref.shape[1]
    y = lax.axis_index("dp")
    e = lax.axis_index("expert")
    t = lax.axis_index("tensor")
    z, c = e // 2, e % 2
    x, yl = t // 2, t % 2
    right, left = (y + 1) % ny, (y + ny - 1) % ny
    sib = {"expert": 2 * z + 1 - c}
    pair = {"tensor": 2 * x + 1 - yl}

    barrier = pltpu.get_barrier_semaphore()

    def greet(device):
        pl.semaphore_signal(barrier, inc=1, device_id=device, device_id_type=MESH)

    greet(sib)
    greet({"dp": right})
    greet({"dp": left})
    greet(pair)
    for d in range(1, nx):
        greet({"tensor": 2 * ((x + d) % nx) + yl})

    def greet_above(i, carry):
        greet({"expert": 2 * i + c})
        return carry

    lax.fori_loop(z + 1, nz, greet_above, 0)

    loads = [
        pltpu.make_async_copy(source, to, load.at[i])
        for i, (source, to) in enumerate(
            [
                (ids_ref, ids_both.at[0]), (prob_ref, prob_both.at[0]), (x_ref, x_both.at[0]),
                (w_ref, w), (gate_ref, gate), (up_ref, up),
            ]
        )
    ]
    for copy in loads:
        copy.start()

    dims = (nz, slab, tok)
    dest = lax.broadcasted_iota(jnp.int32, dims, 0)
    core, expert, rank = row_labels(dims, 1, cap)
    name = 4 * dest + 2 * c + expert
    earlier = (
        lax.broadcasted_iota(jnp.int32, (tok, tok), 0)
        < lax.broadcasted_iota(jnp.int32, (tok, tok), 1)
    ).astype(F32).astype(BF16)

    def pick(i, which):
        mine = core == which
        first = ((name == ids_both[i, 0:1, :].reshape(1, 1, tok)) & mine).astype(F32)
        second = ((name == ids_both[i, 1:2, :].reshape(1, 1, tok)) & mine).astype(F32)
        both = first + second
        count = jnp.dot(
            both.reshape(nz * slab, tok).astype(BF16), earlier, preferred_element_type=F32
        ).reshape(dims)
        here = (count == rank.astype(F32)).astype(F32)
        weight = (
            first * prob_both[i, 0:1, :].reshape(1, 1, tok)
            + second * prob_both[i, 1:2, :].reshape(1, 1, tok)
        ) * here
        return (both * here).reshape(nz * slab, tok).astype(BF16), weight

    loads[0].wait()
    loads[1].wait()
    chosen_a, weight_a = pick(0, c)

    pl.semaphore_wait(barrier, 1 + 2 + 1 + (nx - 1) + z)

    exchange = [
        pltpu.make_async_remote_copy(
            source, to, sib_send.at[i], sib_recv.at[i], device_id=sib, device_id_type=MESH
        )
        for i, (source, to) in enumerate(
            [(ids_ref, ids_both.at[1]), (prob_ref, prob_both.at[1]), (x_ref, x_both.at[1])]
        )
    ]
    for copy in exchange:
        copy.start()

    def answer_below(i, carry):
        pl.semaphore_signal(
            ready.at[z], inc=1, device_id={"expert": 2 * i + c}, device_id_type=MESH
        )
        return carry

    lax.fori_loop(0, z, answer_below, 0)
    exchange[0].wait_recv()
    exchange[1].wait_recv()
    chosen_b, weight_b = pick(1, 1 - c)
    weight = jnp.sum(weight_a + weight_b, axis=2, keepdims=True)
    loads[2].wait()
    exchange[2].wait_recv()
    picked = jnp.dot(
        jnp.concatenate([chosen_a, chosen_b], axis=1), x_both[...].reshape(2 * tok, feat),
        preferred_element_type=F32,
    )
    outbox[...] = (picked.reshape(nz, slab, feat) * weight).astype(BF16)

    def z_to(s, j):
        return (z + s, z + nz - s - 1)[j] % nz

    def z_copy(s, j):
        to = z_to(s, j)
        return pltpu.make_async_remote_copy(
            outbox.at[to], rows.at[y, s, j], z_send.at[s, j], z_recv.at[s, j],
            device_id={"expert": 2 * to + c}, device_id_type=MESH,
        )

    def z_start(s, j):
        to = z_to(s, j)

        @pl.when(to > z)
        def _():
            pl.semaphore_wait(ready.at[to], 1)

        z_copy(s, j).start()

    def y_copy(s, j, side):
        return pltpu.make_async_remote_copy(
            rows.at[y, s, j], rows.at[y, s, j], y_send.at[s, j, side], y_recv.at[s, j, side],
            device_id={"dp": (y + 1 + side * (ny - 2)) % ny}, device_id_type=MESH,
        )

    def f_copy(s, j):
        source, to = ((left, right), (right, left))[j]
        return pltpu.make_async_remote_copy(
            rows.at[source, s, j], rows.at[source, s, j], f_send.at[s, j], f_recv.at[s, j],
            device_id={"dp": to}, device_id_type=MESH,
        )

    def x_copy(s, d):
        to = (x + d) % nx
        return pltpu.make_async_remote_copy(
            part.at[s, to], part_in.at[s, d - 1], x_send.at[s, d - 1], x_recv.at[s, d - 1],
            device_id={"tensor": 2 * to + yl}, device_id_type=MESH,
        )

    def t_copy(m):
        return pltpu.make_async_remote_copy(
            half_out.at[m], half_in.at[m], t_send.at[m], t_recv.at[m],
            device_id=pair, device_id_type=MESH,
        )

    def place(s, j):
        at = (z + nz - s, z + s + 1)[j] % nz
        return at // steps, at % steps

    def spread(s):
        @pl.when(s > 0)
        def _():
            z_copy(s, 0).wait_recv()
            for side in (c, 1 - c):
                y_copy(s, 0, side).start()

        z_copy(s, 1).wait_recv()
        for side in (c, 1 - c):
            y_copy(s, 1, side).start()

    def forward(s):
        for j in range(2):
            y_copy(s, j, j).wait_recv()
            f_copy(s, j).start()

    def multiply(s):
        for j in range(2):
            y_copy(s, j, 1 - j).wait_recv()
        for j in range(2):
            f_copy(s, j).wait_recv()
        block = jnp.concatenate(
            [rows[i, s].astype(F32).reshape(2 * slab, feat) for i in range(ny)], axis=0
        ).astype(BF16)
        contract = (((1,), (1,)), ((), ()))
        a = lax.dot_general(block, w[0], contract, preferred_element_type=F32)
        b = lax.dot_general(block, w[1], contract, preferred_element_type=F32)
        _, which, _ = row_labels((2 * ny, slab, hid), 1, cap)
        value = jnp.where(
            which == 1, b.reshape(2 * ny, slab, hid), a.reshape(2 * ny, slab, hid)
        )
        part[s] = value.astype(BF16).reshape(ny, 2, slab, hid)
        for i in (2, 1, 3):
            x_copy(s, i + c * (nx - 2 * i)).start()

    def reduce(s):
        for d in range(1, nx):
            x_copy(s, d).wait_recv()
        for j in range(2):
            half, m = place(s, j)
            value = part[s, x, j].astype(F32)
            for d in range(nx - 1):
                value = value + part_in[s, d, j].astype(F32)

            @pl.when(half == yl)
            def _():
                own_sum[m] = value

            @pl.when(half != yl)
            def _():
                half_out[m] = value.astype(BF16)
                t_copy(m).start()

    def finish(s):
        for j in range(2):
            half, m = place(s, j)

            @pl.when(half == yl)
            def _():
                t_copy(m).wait_recv()
                upstream = own_sum[m] + half_in[m].astype(F32)
                res_gate[m] = upstream * fac_gate[m]
                res_up[m] = upstream * fac_up[m]

    def drain(s):
        @pl.when(s > 0)
        def _():
            z_copy(s, 0).wait_send()

        z_copy(s, 1).wait_send()
        for j in range(2):
            for side in range(2):
                y_copy(s, j, side).wait_send()
            f_copy(s, j).wait_send()
            half, m = place(s, j)

            @pl.when(half != yl)
            def _():
                t_copy(m).wait_send()

        for d in range(1, nx):
            x_copy(s, d).wait_send()

    rows[y, 0, 0] = outbox[z]
    for side in (c, 1 - c):
        y_copy(0, 0, side).start()
    for s in range(1, min(AHEAD, steps)):
        z_start(jnp.int32(s), 0)
    for s in range(min(AHEAD, steps)):
        z_start(jnp.int32(s), 1)

    col = lax.broadcasted_iota(jnp.int32, (slab, 2 * steps * 2 * cap), 1)
    core2, expert2, rank2 = row_labels(col.shape, 0, cap)
    base = expert2 * (steps * 2 * cap) + core2 * cap + rank2
    order = jnp.concatenate(
        [(col == base + 2 * cap * m).astype(F32) for m in range(steps)], axis=0
    ).astype(BF16)

    def factors():
        def to_slabs(ref):
            return jnp.dot(order, ref[...], preferred_element_type=F32).reshape(steps, slab, hid)

        for copy in loads[3:]:
            copy.wait()
        pre_gate = to_slabs(gate)
        pre_up = to_slabs(up)
        sigma = jax.nn.sigmoid(pre_gate)
        fac_up[...] = pre_gate * sigma
        fac_gate[...] = pre_up * sigma * (1.0 + pre_gate * (1.0 - sigma))

    def step(s, carry):
        @pl.when(s + AHEAD < steps)
        def _():
            z_start(s + AHEAD, 0)
            z_start(s + AHEAD, 1)

        def stage(lag, body):
            @pl.when((s >= lag) & (s < steps + lag))
            def _():
                body(s - lag)

        stage(FORWARD, forward)
        stage(0, spread)

        @pl.when(s == 1)
        def _():
            factors()

        stage(MULTIPLY, multiply)
        stage(REDUCE, reduce)
        stage(FINISH, finish)
        stage(FINISH, drain)
        return carry

    lax.fori_loop(0, steps + FINISH, step, 0)

    def from_slabs(ref):
        value = ref[...].reshape(steps * slab, hid).astype(BF16)
        return lax.dot_general(
            order, value, (((0,), (0,)), ((), ())), preferred_element_type=F32
        ).astype(BF16)

    out_gate_ref[...] = from_slabs(res_gate)
    out_up_ref[...] = from_slabs(res_up)

    for copy in exchange:
        copy.wait_send()


def shards(out_grad, expert_ids, gate_probs, expert_down, saved_gate, saved_up):
    tok, feat = out_grad.shape
    hid = expert_down.shape[1]
    nz = lax.axis_size("expert") // 2
    ny = lax.axis_size("dp")
    nx = lax.axis_size("tensor") // 2
    cap = saved_gate.shape[1] * 2 * nx // (2 * nz * ny)
    steps, slab = nz // 2, 4 * cap
    assert nx == ny and expert_down.shape[0] == 2
    dma = pltpu.SemaphoreType.DMA
    out_rows = 2 * saved_gate.shape[1]
    out = jax.ShapeDtypeStruct((out_rows, hid), BF16)
    vmem = pl.BlockSpec(memory_space=pltpu.VMEM)
    hbm = pl.BlockSpec(memory_space=pl.ANY)
    grad_gate, grad_up = pl.pallas_call(
        functools.partial(kernel, (nz, ny, nx, cap)),
        out_shape=(out, out),
        in_specs=[hbm] * 6,
        out_specs=(vmem, vmem),
        scratch_shapes=[
            pltpu.VMEM((2, tok, feat), BF16),
            pltpu.VMEM((2, 2, tok), jnp.int32),
            pltpu.VMEM((2, 2, tok), F32),
            pltpu.VMEM((2, hid, feat), BF16),
            pltpu.VMEM((out_rows, hid), BF16),
            pltpu.VMEM((out_rows, hid), BF16),
            pltpu.VMEM((nz, slab, feat), BF16),
            pltpu.VMEM((ny, steps, 2, slab, feat), BF16),
            pltpu.VMEM((steps, ny, 2, slab, hid), BF16),
            pltpu.VMEM((steps, nx - 1, 2, slab, hid), BF16),
            pltpu.VMEM((steps, slab, hid), BF16),
            pltpu.VMEM((steps, slab, hid), BF16),
            pltpu.VMEM((steps, slab, hid), F32),
            pltpu.VMEM((steps, slab, hid), F32),
            pltpu.VMEM((steps, slab, hid), F32),
            pltpu.VMEM((steps, slab, hid), F32),
            pltpu.VMEM((steps, slab, hid), F32),
            dma((6,)), dma((3,)), dma((3,)),
            dma((steps, 2)), dma((steps, 2)),
            dma((steps, 2, 2)), dma((steps, 2, 2)),
            dma((steps, 2)), dma((steps, 2)),
            dma((steps, nx - 1)), dma((steps, nx - 1)),
            dma((steps,)), dma((steps,)), pltpu.SemaphoreType.REGULAR((nz,)),
        ],
        compiler_params=pltpu.CompilerParams(
            collective_id=0, has_side_effects=True, vmem_limit_bytes=60 * 1024 * 1024
        ),
    )(
        out_grad, expert_ids.T, gate_probs.T, expert_down,
        saved_gate.reshape(out_rows, hid), saved_up.reshape(out_rows, hid),
    )
    return grad_gate.reshape(saved_gate.shape), grad_up.reshape(saved_up.shape)


def solution(mesh):
    in_specs = (
        P(("dp", "expert"), "tensor"),
        P(("dp", "expert"), None),
        P(("dp", "expert"), None),
        P("expert", "dp", "tensor"),
        P("expert", "tensor", "dp"),
        P("expert", "tensor", "dp"),
    )
    out_specs = (P("expert", "tensor", "dp"), P("expert", "tensor", "dp"))
    return jax.shard_map(shards, mesh=mesh, in_specs=in_specs, out_specs=out_specs, check_vma=False)
```
